32 devices in a mesh: row: 4 (over z), col: 8 (over y, x, core).
Axes of the slice: x: 2, y: 2, z: 4, core: 2. Of those that a mesh axis runs over, the one named last changes fastest.
Arguments:
- amplitudes: bfloat16 [16384, 16384], P('row', 'col'), may hold values from -0.046875 to 0.046875
- accumulated: float32 [16384, 16384], P('row', 'col'), may hold values from -6 to 6
- cholesky: bfloat16 [16384, 1536], P(('row', 'col')), may hold values from -1.5 to 1.5
- occ_index: int32 [16384], replicated, may hold values from 0 to 63
- vir_index: int32 [16384], replicated, may hold values from 0 to 255
- occ_energy: float32 [64], replicated, may hold values from -3 to -0.5
- vir_energy: float32 [256], replicated, may hold values from 0.5 to 4
Outputs:
- updated: float32 [16384, 16384], P('row', 'col')
The draws below stay inside these ranges and needn't reach their ends.
All inputs are finite; a program needn't handle non-finite values.
Results may differ from the reference program's by a relative error of at most 0.0022.
Values may be sent and summed in bfloat16 or wider, within the bound.
A program may use at most 192 MiB of HBM per device.

```python
import jax
import jax.numpy as jnp
from jax import lax

N = 16384
P_SIZE = 1536
NOCC = 64
NVIR = 256


def place_ends(values, key, smallest, largest):
    place = [jax.random.randint(jax.random.fold_in(key, axis), (), 0, length) for axis, length in enumerate(values.shape)]
    longest = values.shape.index(max(values.shape))
    beside = place[:longest] + [(place[longest] + 1) % values.shape[longest]] + place[longest + 1:]
    return values.at[tuple(place)].set(smallest).at[tuple(beside)].set(largest)


def levels(rng, shape, split, smallest, high):
    gain, own = 1.0, jax.random.fold_in(rng, 6)
    for axis_at, parts in split:
        steps = jnp.exp(jax.random.uniform(jax.random.fold_in(own, axis_at), (parts,), jnp.float32, smallest / len(split), high / len(split)))
        gain = gain * jnp.repeat(steps, shape[axis_at] // parts).reshape([-1 if axis == axis_at else 1 for axis in range(len(shape))])
    return gain


def noise(own_key, dims, width, most, shards=(), held_as=jnp.bfloat16):
    values = jax.random.normal(own_key, dims, jnp.float32) * width
    if len(shards) > 0:
        values = levels(own_key, dims, shards, -0.22, 0.18) * values
    return jnp.clip(values, min=-most, max=most).astype(held_as)


def setup_inputs(seed: int = 0) -> dict:
    splits = jax.random.split(jax.random.key(seed), 8)
    return {
        "amplitudes": noise(splits[0], (N, N), N ** -0.5, 0.046875, ((0, 4), (1, 8))),
        "accumulated": noise(splits[1], (N, N), 1.0, 6.0, ((0, 4), (1, 8)), jnp.float32),
        "cholesky": noise(splits[2], (N, P_SIZE), 0.25, 1.5, ((0, 32),)),
        "occ_index": place_ends(jax.random.randint(splits[3], (N,), 0, NOCC), jax.random.fold_in(splits[3], 1), 0, NOCC - 1).astype(jnp.int32),
        "vir_index": place_ends(jax.random.randint(splits[4], (N,), 0, NVIR), jax.random.fold_in(splits[4], 1), 0, NVIR - 1).astype(jnp.int32),
        "occ_energy": jnp.clip(jax.random.uniform(splits[5], (NOCC,), jnp.float32, -3.0, -0.5), -3.0, -0.5),
        "vir_energy": jnp.clip(jax.random.uniform(splits[6], (NVIR,), jnp.float32, 0.5, 4.0), 0.5, 4.0),
    }


def lookup(index, table):
    hits = index[:, None] == jnp.arange(table.shape[0], dtype=jnp.int32)[None, :]
    return jnp.sum(jnp.where(hits, table[None, :], jnp.zeros((), table.dtype)), axis=1)


def reference(amplitudes, accumulated, cholesky, occ_index, vir_index, occ_energy, vir_energy):
    tb = jnp.dot(amplitudes, cholesky, preferred_element_type=jnp.float32)
    dressed = (cholesky.astype(jnp.float32) + tb).astype(jnp.bfloat16)
    gap = lookup(occ_index, occ_energy) - lookup(vir_index, vir_energy)
    blocks = 16
    block_rows = N // blocks
    acc_blocks = accumulated.reshape(blocks, block_rows, N)
    x_blocks = dressed.reshape(blocks, block_rows, P_SIZE)
    gap_blocks = gap.reshape(blocks, block_rows)

    def one_block(items):
        acc_part, x_part, gap_part = items
        product = lax.dot_general(x_part, dressed, (((1,), (1,)), ((), ())), preferred_element_type=jnp.float32)
        return acc_part + product / (gap_part[:, None] + gap[None, :])

    result = lax.map(one_block, (acc_blocks, x_blocks, gap_blocks))
    return result.reshape(N, N)
```

```python
import jax
import jax.numpy as jnp
from jax import lax
from jax.sharding import PartitionSpec as P


def lookup(index, table):
    hits = index[:, None] == jnp.arange(table.shape[0], dtype=jnp.int32)[None, :]
    return jnp.sum(jnp.where(hits, table[None, :], jnp.zeros((), table.dtype)), axis=1)


def chunk_bounds(width):
    count = 3 if width % 384 == 0 else 1
    step = width // count
    return [(at * step, step) for at in range(count)]


def after(value, *earlier):
    return lax.optimization_barrier((value, *earlier))[0]


def along_rows(piece, row_count):
    held = [piece]
    for shift in range(1, row_count):
        pairs = [(r, (r + shift) % row_count) for r in range(row_count)]
        held.append(lax.ppermute(piece, "row", pairs))
    return held


def to_columns(held, row_count, col_count):
    ratio = col_count // row_count
    row_rank = lax.axis_index("row")
    col_rank = lax.axis_index("col")
    size, width = held[0].shape
    out = jnp.zeros((row_count * size, width), held[0].dtype)
    for turn in range(row_count):
        wanted = (col_rank % row_count - turn) % row_count
        send = lax.select_n((row_rank - wanted) % row_count, *held)
        pairs = [
            ((c % ratio) * row_count + (c // ratio + turn) % row_count, c)
            for c in range(col_count)
        ]
        got = lax.ppermute(send, "col", pairs)
        place = (col_rank // ratio + turn) % row_count
        out = lax.dynamic_update_slice_in_dim(out, got, place * size, 0)
    return out


def on_device(amplitudes, accumulated, cholesky, occ_index, vir_index, occ_energy, vir_energy):
    row_count = lax.axis_size("row")
    col_count = lax.axis_size("col")
    row_rank = lax.axis_index("row")
    col_rank = lax.axis_index("col")
    row_block = amplitudes.shape[0]
    col_block = amplitudes.shape[1]
    size = cholesky.shape[0]

    upward = [1 << bit for bit in range(1, col_count.bit_length() - 1)]
    downward = upward[::-1]
    levels = len(upward)
    even = col_rank % 2 == 0

    def block_of(base, from_up, slot):
        mask = 0
        for level in range(levels):
            if slot >> (levels - 1 - level) & 1:
                mask = mask + jnp.where(from_up, upward[level], downward[level])
        return base ^ mask

    def rows_of(block):
        return lax.dynamic_slice_in_dim(amplitudes, block * size, size, 0)

    slots = range(1 << levels)
    half = len(slots) // 2
    other = col_rank ^ 1
    t_send = jnp.concatenate([rows_of(block_of(other, ~even, s)) for s in slots], 0)
    t_pass = jnp.concatenate([rows_of(block_of(col_rank, even, s)) for s in slots[half:]], 0)
    t_keep = jnp.concatenate([rows_of(block_of(col_rank, even, s)) for s in slots[:half]], 0)
    core_pairs = [(c, c ^ 1) for c in range(col_count)]

    def sums(b_part, at_core, at_last):
        def dot(rows):
            return jnp.dot(rows, b_part, preferred_element_type=jnp.float32)

        came = lax.ppermute(dot(t_send), "col", core_pairs)
        came = after(came, *at_core)
        b_part = after(b_part, came)
        send = dot(t_pass) + came[half * size :]
        total = dot(t_keep) + came[: half * size]
        for level in range(levels):
            if level > 0:
                middle = total.shape[0] // 2
                send, total = total[middle:], total[:middle]
            pairs = [
                (c, c ^ (upward[level] if c % 2 == 0 else downward[level]))
                for c in range(col_count)
            ]
            if level == levels - 1:
                send = after(send, *at_last)
            total = total + lax.ppermute(send, "col", pairs)
        return total, came

    occ_rows = lax.dynamic_slice_in_dim(occ_index, row_rank * row_block, row_block, 0)
    vir_rows = lax.dynamic_slice_in_dim(vir_index, row_rank * row_block, row_block, 0)
    occ_cols = lax.dynamic_slice_in_dim(occ_index, col_rank * col_block, col_block, 0)
    vir_cols = lax.dynamic_slice_in_dim(vir_index, col_rank * col_block, col_block, 0)
    gap_rows = lookup(occ_rows, occ_energy) - lookup(vir_rows, vir_energy)
    gap_cols = lookup(occ_cols, occ_energy) - lookup(vir_cols, vir_energy)

    chols, b_held = [], []
    for start, width in chunk_bounds(cholesky.shape[1]):
        chol = cholesky[:, start : start + width]
        chols.append(chol)
        first = after(chol, *b_held[-1]) if b_held else chol
        b_held.append(along_rows(first, row_count))

    came, x_held, x_rows, x_cols = None, [], [], []
    for at, chol in enumerate(chols):
        held = b_held[at]
        if at > 0:
            held = lax.optimization_barrier((*held, came))[: len(held)]
        b_cols = to_columns(held, row_count, col_count)
        if at > 0:
            b_cols = after(b_cols, x_held[-1][0])
        elif len(chols) > 1:
            b_cols = after(b_cols, *b_held[1])
        beside = x_held[-1] if at > 0 else b_held[min(2, len(chols) - 1)]
        at_last = beside[2:] + (x_rows[-1:] if at > 0 else [])
        summed, came = sums(b_cols, beside[1:2], at_last)
        x_piece = (chol.astype(jnp.float32) + summed).astype(jnp.bfloat16)
        if at > 1:
            x_piece = after(x_piece, x_cols[at - 2])
        x_rows.append(lax.all_gather(x_piece, "col", axis=0, tiled=True))
        x_held.append(along_rows(x_piece, row_count))
        x_cols.append(to_columns(x_held[-1], row_count, col_count))

    product = None
    for rows, cols in zip(x_rows, x_cols):
        term = lax.dot_general(
            rows, cols, (((1,), (1,)), ((), ())), preferred_element_type=jnp.float32
        )
        product = term if product is None else product + term
    return accumulated + product / (gap_rows[:, None] + gap_cols[None, :])


def solution(mesh):
    in_specs = (P("row", "col"), P("row", "col"), P(("row", "col"), None), P(), P(), P(), P())
    out_specs = P("row", "col")
    return jax.shard_map(
        on_device, mesh=mesh, in_specs=in_specs, out_specs=out_specs, check_vma=False
    )
```

```python
import jax
import jax.numpy as jnp
from jax import lax
from jax.sharding import PartitionSpec as P


def lookup(index, table):
    hits = index[:, None] == jnp.arange(table.shape[0], dtype=jnp.int32)[None, :]
    return jnp.sum(jnp.where(hits, table[None, :], jnp.zeros((), table.dtype)), axis=1)


def chunk_bounds(width):
    unit = width // 6
    if width % 6 or unit % 128:
        return [(0, width)]
    return [(0, unit), (unit, 2 * unit), (3 * unit, 2 * unit), (5 * unit, unit)]


def after(value, *earlier):
    return lax.optimization_barrier((value, *earlier))[0]


def along_rows(piece, row_count):
    held = [piece]
    for shift in range(1, row_count):
        pairs = [(r, (r + shift) % row_count) for r in range(row_count)]
        held.append(lax.ppermute(piece, "row", pairs))
    return held


def to_columns(held, row_count, col_count):
    ratio = col_count // row_count
    row_rank = lax.axis_index("row")
    col_rank = lax.axis_index("col")
    size, width = held[0].shape
    out = jnp.zeros((row_count * size, width), held[0].dtype)
    for turn in range(row_count):
        wanted = (col_rank % row_count - turn) % row_count
        send = lax.select_n((row_rank - wanted) % row_count, *held)
        pairs = [
            ((c % ratio) * row_count + (c // ratio + turn) % row_count, c)
            for c in range(col_count)
        ]
        got = lax.ppermute(send, "col", pairs)
        place = (col_rank // ratio + turn) % row_count
        out = lax.dynamic_update_slice_in_dim(out, got, place * size, 0)
    return out


def on_device(amplitudes, accumulated, cholesky, occ_index, vir_index, occ_energy, vir_energy):
    row_count = lax.axis_size("row")
    col_count = lax.axis_size("col")
    row_rank = lax.axis_index("row")
    col_rank = lax.axis_index("col")
    row_block = amplitudes.shape[0]
    col_block = amplitudes.shape[1]
    size = cholesky.shape[0]

    upward = [1 << bit for bit in range(1, col_count.bit_length() - 1)]
    downward = upward[::-1]
    levels = len(upward)
    even = col_rank % 2 == 0

    def block_of(base, from_up, slot):
        mask = 0
        for level in range(levels):
            if slot >> (levels - 1 - level) & 1:
                mask = mask + jnp.where(from_up, upward[level], downward[level])
        return base ^ mask

    def rows_of(block):
        return lax.dynamic_slice_in_dim(amplitudes, block * size, size, 0)

    slots = range(1 << levels)
    half = len(slots) // 2
    other = col_rank ^ 1
    t_send = jnp.concatenate([rows_of(block_of(other, ~even, s)) for s in slots], 0)
    t_pass = jnp.concatenate([rows_of(block_of(col_rank, even, s)) for s in slots[half:]], 0)
    t_keep = jnp.concatenate([rows_of(block_of(col_rank, even, s)) for s in slots[:half]], 0)
    core_pairs = [(c, c ^ 1) for c in range(col_count)]

    def dot(rows, b_part):
        return jnp.dot(rows, b_part, preferred_element_type=jnp.float32)

    occ_rows = lax.dynamic_slice_in_dim(occ_index, row_rank * row_block, row_block, 0)
    vir_rows = lax.dynamic_slice_in_dim(vir_index, row_rank * row_block, row_block, 0)
    occ_cols = lax.dynamic_slice_in_dim(occ_index, col_rank * col_block, col_block, 0)
    vir_cols = lax.dynamic_slice_in_dim(vir_index, col_rank * col_block, col_block, 0)
    gap_rows = lookup(occ_rows, occ_energy) - lookup(vir_rows, vir_energy)
    gap_cols = lookup(occ_cols, occ_energy) - lookup(vir_cols, vir_energy)

    chols = [cholesky[:, at : at + width] for at, width in chunk_bounds(cholesky.shape[1])]
    count = len(chols)
    b_held = []
    for chol in chols:
        first = after(chol, *b_held[-1]) if b_held else chol
        b_held.append(along_rows(first, row_count))

    x_held, x_rows, x_cols = [], [], []
    b_cols = to_columns(b_held[0], row_count, col_count)
    if count > 1:
        b_cols = after(b_cols, b_held[1][1])
    sent = dot(t_send, b_cols)
    for at, chol in enumerate(chols):
        beside = x_held[-1] if at > 0 else []
        came = lax.ppermute(sent, "col", core_pairs)
        b_next = None
        if at + 1 < count:
            held = b_held[at + 1]
            held = lax.optimization_barrier((*held, came))[: len(held)]
            b_next = to_columns(held, row_count, col_count)
        b_cols = after(b_cols, came)
        send = dot(t_pass, b_cols) + came[half * size :]
        total = dot(t_keep, b_cols) + came[: half * size]
        for level in range(levels):
            if level > 0:
                middle = total.shape[0] // 2
                send, total = total[middle:], total[:middle]
            if level == levels - 1:
                send = after(send, *beside[1:2])
                if at > 0:
                    send = after(send, x_rows[at - 1])
                if at + 2 < count:
                    send = after(send, b_held[at + 2][1])
                if b_next is not None:
                    send = after(send, b_next)
            pairs = [
                (c, c ^ (upward[level] if c % 2 == 0 else downward[level]))
                for c in range(col_count)
            ]
            total = total + lax.ppermute(send, "col", pairs)
        x_piece = (chol.astype(jnp.float32) + total).astype(jnp.bfloat16)
        x_piece = after(x_piece, *beside[2:])
        if at > 1:
            x_piece = after(x_piece, x_cols[at - 2])
        if b_next is not None:
            b_cols = b_next
            sent = dot(t_send, b_cols)
            x_piece = after(x_piece, sent)
        x_rows.append(lax.all_gather(x_piece, "col", axis=0, tiled=True))
        x_held.append(along_rows(x_piece, row_count))
        if at + 1 < count or count < 3:
            x_cols.append(to_columns(x_held[-1], row_count, col_count))

    def product_of(first, last):
        return lax.dot_general(
            jnp.concatenate(x_rows[first:last], 1),
            jnp.concatenate(x_cols[first:last], 1),
            (((1,), (1,)), ((), ())),
            preferred_element_type=jnp.float32,
        )

    if count < 3:
        product = product_of(0, count)
    else:
        product = product_of(0, count - 2)
        held = lax.optimization_barrier((*x_held[-1], product))
        x_cols.append(to_columns(held[:-1], row_count, col_count))
        product = held[-1] + product_of(count - 2, count - 1)
        product = product + product_of(count - 1, count)
    return accumulated + product / (gap_rows[:, None] + gap_cols[None, :])


def solution(mesh):
    in_specs = (P("row", "col"), P("row", "col"), P(("row", "col"), None), P(), P(), P(), P())
    out_specs = P("row", "col")
    return jax.shard_map(
        on_device, mesh=mesh, in_specs=in_specs, out_specs=out_specs, check_vma=False
    )
```
